32 devices in a mesh: area: 4 (over x, core), local: 8 (over z, y).
Axes of the slice: x: 2, y: 2, z: 4, core: 2. Of those that a mesh axis runs over, the one named last changes fastest.
Arguments:
- rates_init: float32 [32, 16384], P(None, ('area', 'local')), may hold values from -1 to 1
- drive: float32 [32, 16384], P(None, ('area', 'local')), may hold values from -4 to 4
- within_w: bfloat16 [16384, 4096], P(('area', 'local')), may hold values from -0.125 to 0.125
- long_w: bfloat16 [128, 16, 128, 128], P(('area', 'local')), may hold values from -0.1875 to 0.1875
- columns: int32 [128, 16], P(('area', 'local')), may hold values from 0 to 127, as said below
- area_map: int32 [4], replicated, may hold values from 0 to 3, each once
- counts: int32 [4], replicated, may hold values from 9 to 32, as said below
Outputs:
- rates: float32 [32, 16384], P(None, ('area', 'local'))
The draws below stay inside these ranges and needn't reach their ends.
Inputs may be any that keep to these rules, and one draw needn't show every extreme that they name: `columns`: each device's 4 * 16 entries name populations of any one logical area (entry // 32) at most 32 times, and exactly 32 times for some area. `counts`: some area has all 32 populations present, and some other area has exactly 9.
All inputs are finite; a program needn't handle non-finite values.
Results may differ from the reference program's by a relative error of at most 0.0031.
Values may be sent and summed in bfloat16 or wider, within the bound.
No kernel may reach another device: no remote copies, remote signals or barrier semaphores. Data moves between devices by JAX's collectives and lax.ppermute only.
A program may use at most 64 MiB of HBM per device.

```python
import jax
import jax.numpy as jnp
from jax import lax

POP = 128
COND = 32
P_DEV = 4
KBLK = 16
STEPS = 2
AREAS = 4
GROUP = 8
P_AREA = 32
AREA_N = 4096
NPOP = 128
CAP = 32


def draw_columns(key, part):
    key = jax.random.fold_in(key, 11)
    many = P_DEV * KBLK
    slots = AREAS * CAP

    def one_device(sub):
        first, second, third, fourth = jax.random.split(sub, 4)
        ordinal = jnp.arange(slots, dtype=jnp.int32)
        score = jax.random.randint(first, (slots,), 0, slots) * slots + ordinal
        hot = jax.random.randint(second, (), 0, AREAS)
        score = jnp.where(ordinal // CAP == hot, ordinal - 2 * slots * slots, score)
        chosen = jnp.argsort(score)[:many]
        areas = (chosen // CAP).astype(jnp.int32)
        areas = areas[jax.random.permutation(third, many)]
        pops = jax.random.randint(fourth, (many,), 0, P_AREA)
        return (areas * P_AREA + pops).reshape(P_DEV, KBLK).astype(jnp.int32)
    keys = jax.random.split(key, AREAS * GROUP)
    return jax.vmap(one_device)(keys).reshape(NPOP, KBLK)


def draw_counts(key, part):
    key = jax.random.fold_in(key, 5)
    first, second = jax.random.split(key)
    least = P_AREA // 4 + 1
    values = jax.random.randint(first, (AREAS,), least, P_AREA + 1)
    hot = jax.random.randint(second, (), 0, AREAS)
    cold = (hot + 1) % AREAS
    area_ids = jnp.arange(AREAS)
    values = jnp.where(area_ids == cold, least, values)
    return jnp.where(area_ids == hot, P_AREA, values).astype(jnp.int32)


def level_of(rng, shape, cuts, smallest, top_value):
    def one(axis_at, shards_of):
        steps = jax.random.uniform(jax.random.fold_in(jax.random.fold_in(rng, 6), axis_at), (shards_of,), jnp.float32, smallest / len(cuts), top_value / len(cuts))
        return jnp.repeat(jnp.exp(steps), shape[axis_at] // shards_of).reshape((-1,) + (1,) * (len(shape) - axis_at - 1))

    gain = one(*cuts[0])
    for cut in cuts[1:]:
        gain = gain * one(*cut)
    return gain


def normal_values(rng, dims, width, limit, cuts=(), kind=jnp.bfloat16):
    loudness = level_of(rng, dims, cuts, -0.22, 0.18) if cuts else 1.0
    drawn = jax.random.normal(rng, dims, jnp.float32) * width * loudness
    return jnp.minimum(jnp.maximum(drawn, -limit), limit).astype(kind)


def setup_inputs(seed: int = 0) -> dict:
    seeds = jax.random.split(jax.random.key(seed), 8)
    return {
        "rates_init": jnp.clip(jax.random.uniform(seeds[0], (COND, NPOP * POP), jnp.float32, -1.0, 1.0) * level_of(seeds[0], (COND, NPOP * POP), ((1, 32),), -0.4, 0.0), -1.0, 1.0),
        "drive": normal_values(seeds[1], (COND, NPOP * POP), 0.7, 4.0, ((1, 32),), jnp.float32),
        "within_w": normal_values(seeds[2], (NPOP * POP, AREA_N), (AREA_N // 2) ** -0.5, 0.125, ((0, 32),)),
        "long_w": normal_values(seeds[3], (NPOP, KBLK, POP, POP), (KBLK * POP // 2) ** -0.5, 0.1875, ((0, 32),)),
        "columns": draw_columns(jax.random.fold_in(seeds[7], 71), 0),
        "area_map": jax.random.permutation(seeds[5], AREAS).astype(jnp.int32),
        "counts": draw_counts(jax.random.fold_in(seeds[7], 71), 0),
    }


def reference(rates_init, drive, within_w, long_w, columns, area_map, counts):
    slot_index = jnp.arange(NPOP, dtype=jnp.int32)
    mesh_area = slot_index // P_AREA
    present_pop = ((slot_index % P_AREA) < counts[mesh_area]).astype(jnp.float32)
    present = jnp.repeat(present_pop, POP)[None, :]
    rates = rates_init * present
    source = area_map[columns // P_AREA] * P_AREA + columns % P_AREA
    weights3 = within_w.reshape(AREAS, AREA_N, AREA_N)
    long4 = long_w.reshape(AREAS, P_AREA, KBLK, POP, POP)
    source3 = source.reshape(AREAS, P_AREA, KBLK)
    for step in range(STEPS):
        rounded = rates.astype(jnp.bfloat16)
        by_area = rounded.reshape(COND, AREAS, AREA_N)

        def inner_one(index):
            part = lax.dynamic_index_in_dim(by_area, index, 1, keepdims=False)
            return jnp.dot(part, weights3[index].T, preferred_element_type=jnp.float32)

        inner = lax.map(inner_one, jnp.arange(AREAS, dtype=jnp.int32))
        inner = jnp.transpose(inner, (1, 0, 2)).reshape(COND, NPOP * POP)
        pops3 = rounded.reshape(COND, NPOP, POP)

        def outer_one(index):
            picked = jnp.take(pops3, source3[index].reshape(-1), axis=1).reshape(COND, P_AREA, KBLK, POP)
            return jnp.einsum("cpkj,pkij->cpi", picked.astype(jnp.float32), long4[index].astype(jnp.float32))

        outer = lax.map(outer_one, jnp.arange(AREAS, dtype=jnp.int32))
        outer = jnp.transpose(outer, (1, 0, 2, 3)).reshape(COND, NPOP * POP)
        rates = jnp.tanh(inner + outer + drive) * present
    return rates
```

```python
import functools

import jax
import jax.numpy as jnp
from jax import lax
from jax.experimental import pallas as pl
from jax.experimental.pallas import tpu as pltpu
from jax.sharding import PartitionSpec as P

STEPS = 2
CORES = 2
AXES = ("area", "local")
VMEM = pl.BlockSpec(memory_space=pltpu.VMEM)
SMEM = pl.BlockSpec(memory_space=pltpu.SMEM)


def call(kernel, out, operands, specs, flops, scratch=(), trans=0):
    moved = sum(x.size * x.dtype.itemsize for x in operands)
    return pl.pallas_call(
        kernel,
        out_shape=out,
        in_specs=specs,
        out_specs=VMEM,
        scratch_shapes=scratch,
        compiler_params=pltpu.CompilerParams(vmem_limit_bytes=40 * 2**20),
        cost_estimate=pl.CostEstimate(
            flops=flops, bytes_accessed=moved, transcendentals=trans
        ),
    )(*operands)


def present_of(s, p_dev, counts_ref):
    here = lax.axis_index("local") * p_dev + s
    return jnp.where(here < counts_ref[lax.axis_index("area")], 1.0, 0.0)


def first_kernel(p_dev, pop, counts_ref, x_ref, out_ref):
    for s in range(p_dev):
        at = slice(s * pop, (s + 1) * pop)
        out_ref[:, at] = (x_ref[:, at] * present_of(s, p_dev, counts_ref)).astype(
            out_ref.dtype
        )


def inner_kernel(lsub, other, cond, *refs):
    blocks_ref, w_ref = refs[0], refs[1]
    out_ref = refs[-1]
    here = lax.axis_index("local")
    width = blocks_ref.shape[1]
    total = refs[2][...] if len(refs) == 4 else None
    for d in range(blocks_ref.shape[0] // cond):
        l = here ^ (d * lsub + other)
        at = pl.ds(pl.multiple_of(l * width, width), width)
        part = lax.dot_general(
            blocks_ref[d * cond : (d + 1) * cond, :],
            w_ref[:, at],
            (((1,), (1,)), ((), ())),
            preferred_element_type=jnp.float32,
        )
        total = part if total is None else total + part
    out_ref[...] = total


def outer_kernel(shape, n_arrays, *refs):
    nx, l1, l2, p_dev, pop, kblk, cond = shape
    counts_ref, map_ref, columns_ref, w_ref, inner_ref, drive_ref = refs[:6]
    arrays = refs[6 : 6 + n_arrays]
    out_ref, table = refs[-2:]
    per = l1 * p_dev
    for n, a in enumerate(arrays):
        for d in range(l1):
            for s in range(p_dev):
                table[n * per + d * p_dev + s] = a[
                    d * cond : (d + 1) * cond, s * pop : (s + 1) * pop
                ]
    area = lax.axis_index("area")
    local = lax.axis_index("local")
    p_area = l1 * l2 * p_dev
    for p in range(p_dev):
        total = None
        for k in range(kblk):
            column = columns_ref[p, k]
            da = map_ref[column // p_area] ^ area
            inside = column % p_area
            dl = (inside // p_dev) ^ local
            n = ((da % CORES) * nx + da // CORES) * l2 + dl % l2
            at = n * per + (dl // l2) * p_dev + inside % p_dev
            part = lax.dot_general(
                table[at],
                w_ref[p, k],
                (((1,), (1,)), ((), ())),
                preferred_element_type=jnp.float32,
            )
            total = part if total is None else total + part
        here = slice(p * pop, (p + 1) * pop)
        rates = jnp.tanh(inner_ref[:, here] + total + drive_ref[:, here])
        out_ref[:, here] = (rates * present_of(p, p_dev, counts_ref)).astype(
            out_ref.dtype
        )


def body(rates_init, drive, within_w, long_w, columns, area_map, counts):
    areas, locs = lax.axis_size("area"), lax.axis_size("local")
    nx, l1 = areas // CORES, 4
    l2 = locs // l1
    p_dev, kblk, pop, _ = long_w.shape
    cond, width = rates_init.shape
    count = areas * locs

    def swap(x, dx=0, dc=0, d1=0, d2=0):
        by = (dx * CORES + dc) * locs + d1 * l2 + d2
        return lax.ppermute(x, AXES, [(i, i ^ by) for i in range(count)])

    mine = call(
        functools.partial(first_kernel, p_dev, pop),
        jax.ShapeDtypeStruct((cond, width), jnp.bfloat16),
        (counts, rates_init),
        [SMEM, VMEM],
        cond * width,
    )
    for step in range(STEPS):
        column = jnp.concatenate(
            [mine] + [swap(mine, d1=d) for d in range(1, l1)], axis=0
        )
        got = {
            (dx, d2): swap(column, dx=dx, d2=d2) if dx or d2 else column
            for dx in range(nx)
            for d2 in range(l2)
        }
        inner = None
        for d2 in range(l2):
            operands = [got[0, d2], within_w] + ([] if inner is None else [inner])
            inner = call(
                functools.partial(inner_kernel, l2, d2, cond),
                jax.ShapeDtypeStruct((cond, width), jnp.float32),
                operands,
                [VMEM] * len(operands),
                2 * cond * width * width * l1,
            )
        arrays = [got[dx, d2] for dx in range(nx) for d2 in range(l2)]
        arrays += [swap(x, dc=1) for x in arrays]
        last = step == STEPS - 1
        mine = call(
            functools.partial(
                outer_kernel, (nx, l1, l2, p_dev, pop, kblk, cond), len(arrays)
            ),
            jax.ShapeDtypeStruct((cond, width), jnp.float32 if last else jnp.bfloat16),
            [counts, area_map, columns, long_w, inner, drive] + arrays,
            [SMEM] * 3 + [VMEM] * (3 + len(arrays)),
            2 * cond * width * kblk * pop,
            scratch=[
                pltpu.VMEM((len(arrays) * l1 * p_dev, cond, pop), jnp.bfloat16)
            ],
            trans=cond * width,
        )
    return mine


def solution(mesh):
    in_specs = (
        P(None, AXES),
        P(None, AXES),
        P(AXES, None),
        P(AXES, None, None, None),
        P(AXES, None),
        P(),
        P(),
    )
    return jax.shard_map(
        body, mesh=mesh, in_specs=in_specs, out_specs=P(None, AXES), check_vma=False
    )
```

```python
import functools

import jax
import jax.numpy as jnp
from jax import lax
from jax.experimental import pallas as pl
from jax.experimental.pallas import tpu as pltpu
from jax.sharding import PartitionSpec as P

STEPS = 2
CORES = 2
AXES = ("area", "local")
VMEM = pl.BlockSpec(memory_space=pltpu.VMEM)
HBM = pl.BlockSpec(memory_space=pltpu.HBM)
DIMS = (((1,), (1,)), ((), ()))


def call(kernel, out, operands, in_specs, flops, scratch=(), out_specs=VMEM, room=24):
    moved = sum(x.size * x.dtype.itemsize for x in operands)
    return pl.pallas_call(
        kernel,
        out_shape=out,
        in_specs=in_specs,
        out_specs=out_specs,
        scratch_shapes=scratch,
        compiler_params=pltpu.CompilerParams(vmem_limit_bytes=room * 2**20),
        cost_estimate=pl.CostEstimate(
            flops=flops, bytes_accessed=moved, transcendentals=0
        ),
    )(*operands)


def in_hbm(x):
    return pltpu.with_memory_space_constraint(x, pltpu.HBM)


def log2(n):
    bits = n.bit_length() - 1
    assert n == 1 << bits
    return bits


def fetch(sources, copies, sems):
    moves = []
    for a, b in zip(sources, copies):
        pieces = 4 if a.ndim > 1 and a.shape[0] >= 256 else 1
        rows = a.shape[0] // pieces
        for n in range(pieces):
            at = pl.ds(n * rows, rows)
            moves.append(
                pltpu.make_async_copy(a.at[at], b.at[at], sems.at[len(moves)])
            )
    for move in moves:
        move.start()
    return moves


def within_kernel(x_ref, w_ref, out_ref, again_ref, sems):
    moves = fetch([w_ref], [out_ref], sems)
    again_ref[...] = x_ref[...]
    for move in moves:
        move.wait()


def long_kernel(sizes, *refs):
    nx, l1, l2, p_dev = sizes
    x_ref, sources, copies = refs[0], refs[1:5], refs[5:7]
    slots_ref, again_ref, columns_ref, map_ref, sems = refs[7:]
    moves = fetch(sources, (columns_ref, map_ref, *copies), sems)
    again_ref[...] = x_ref[...]
    moves[0].wait()
    moves[1].wait()
    area, local = lax.axis_index("area"), lax.axis_index("local")
    inside_bits = log2(l1 * l2 * p_dev)
    columns = columns_ref[...]
    logical = columns >> inside_bits
    inside = columns & ((1 << inside_bits) - 1)
    target = jnp.zeros_like(columns)
    for a in range(nx * CORES):
        target = jnp.where(logical == a, map_ref[a], target)
    da = target ^ area
    dl = (inside >> log2(p_dev)) ^ local
    n = (da & (CORES - 1)) * nx + (da >> log2(CORES))
    n = n * l2 + (dl & (l2 - 1))
    n = n * l1 + (dl >> log2(l2))
    slots_ref[...] = n * p_dev + (inside & (p_dev - 1))
    for move in moves[2:]:
        move.wait()


def count_of(counts_ref):
    count = counts_ref[0]
    for a in range(1, counts_ref.shape[0]):
        count = jnp.where(lax.axis_index("area") == a, counts_ref[a], count)
    return count


def column_kernel(l2, p_dev, pop, counts_ref, *refs):
    out_ref = refs[-1]
    cond = refs[0].shape[0]
    count = count_of(counts_ref)
    for d, block in enumerate(refs[:-1]):
        first = (lax.axis_index("local") ^ (d * l2)) * p_dev
        for s in range(p_dev):
            at = slice(s * pop, (s + 1) * pop)
            x = block[:, at]
            out_ref[d * cond : (d + 1) * cond, at] = jnp.where(
                first + s < count, x, jnp.zeros_like(x)
            )


def inner_kernel(l2, other, cond, *refs):
    blocks_ref, w_ref = refs[:2]
    here = lax.axis_index("local")
    width = blocks_ref.shape[1]
    total = None
    if other:
        total, out_ref = refs[2][...], refs[3]
    else:
        out_ref, again_ref = refs[2:]
        again_ref[...] = blocks_ref[...]
    for d in range(blocks_ref.shape[0] // cond):
        l = here ^ (d * l2 + other)
        at = pl.ds(pl.multiple_of(l * width, width), width)
        part = lax.dot_general(
            blocks_ref[d * cond : (d + 1) * cond, :],
            w_ref[:, at],
            DIMS,
            preferred_element_type=jnp.float32,
        )
        total = part if total is None else total + part
    out_ref[...] = total


def outer_kernel(sizes, n_arrays, *refs):
    l1, p_dev, pop, kblk, cond = sizes
    counts_ref, slots_ref, w_ref, inner_ref, drive_ref = refs[:5]
    arrays = refs[5 : 5 + n_arrays]
    out_ref, table = refs[-2:]
    per = l1 * p_dev
    for n, a in enumerate(arrays):
        for d in range(l1):
            for s in range(p_dev):
                table[n * per + d * p_dev + s] = a[
                    d * cond : (d + 1) * cond, s * pop : (s + 1) * pop
                ]
    count = count_of(counts_ref)
    first = lax.axis_index("local") * p_dev
    for p in range(p_dev):
        picked = jnp.concatenate([table[slots_ref[p, k]] for k in range(kblk)], axis=1)
        weights = jnp.concatenate([w_ref[p, k] for k in range(kblk)], axis=1)
        outer = lax.dot_general(
            picked, weights, DIMS, preferred_element_type=jnp.float32
        )
        here = slice(p * pop, (p + 1) * pop)
        rates = jnp.tanh(inner_ref[:, here] + outer + drive_ref[:, here])
        present = jnp.where(first + p < count, 1.0, 0.0)
        out_ref[:, here] = (rates * present).astype(out_ref.dtype)


def body(rates_init, drive, within_w, long_w, columns, area_map, counts):
    areas, locs = lax.axis_size("area"), lax.axis_size("local")
    nx, l1 = areas // CORES, 4
    l2 = locs // l1
    p_dev, kblk, pop, _ = long_w.shape
    cond, width = rates_init.shape
    devices = areas * locs

    def swap(x, dx=0, dc=0, d1=0, d2=0):
        by = (dx * CORES + dc) * locs + d1 * l2 + d2
        return lax.ppermute(x, AXES, [(i, i ^ by) for i in range(devices)])

    mine = rates_init.astype(jnp.bfloat16)
    shape = jax.ShapeDtypeStruct
    within_w, kept = call(
        within_kernel,
        [pltpu.VMEM(x.shape, x.dtype) for x in (within_w, mine)],
        [mine, in_hbm(within_w)],
        [VMEM, HBM],
        0,
        scratch=[pltpu.SemaphoreType.DMA((4,))],
        out_specs=[VMEM] * 2,
    )
    for step in range(STEPS):
        blocks = [kept] + [swap(mine, d1=d) for d in range(1, l1)]
        column = call(
            functools.partial(column_kernel, l2, p_dev, pop),
            shape((l1 * cond, width), mine.dtype),
            [counts] + blocks,
            [VMEM] * (1 + l1),
            0,
        )
        got = {
            (dx, d2): swap(column, dx=dx, d2=d2) if dx or d2 else column
            for dx in range(nx)
            for d2 in range(l2)
        }
        if step == 0:
            long_w, drive, slots, got[0, 0] = call(
                functools.partial(long_kernel, (nx, l1, l2, p_dev)),
                [
                    pltpu.VMEM(x.shape, x.dtype)
                    for x in (long_w, drive, columns, column)
                ],
                [column] + [in_hbm(x) for x in (columns, area_map, long_w, drive)],
                [VMEM] + [HBM] * 4,
                0,
                scratch=[
                    pltpu.VMEM(columns.shape, columns.dtype),
                    pltpu.VMEM(area_map.shape, area_map.dtype),
                    pltpu.SemaphoreType.DMA((7,)),
                ],
                out_specs=[VMEM] * 4,
            )
        partial = shape((cond, width), jnp.float32)
        flops = 2 * cond * width * width * l1
        inner, got[0, 0] = call(
            functools.partial(inner_kernel, l2, 0, cond),
            [partial, shape(column.shape, column.dtype)],
            (got[0, 0], within_w),
            [VMEM] * 2,
            flops,
            out_specs=[VMEM] * 2,
        )
        for d2 in range(1, l2):
            inner = call(
                functools.partial(inner_kernel, l2, d2, cond),
                partial,
                (got[0, d2], within_w, inner),
                [VMEM] * 3,
                flops,
            )
        arrays = [got[dx, d2] for dx in range(nx) for d2 in range(l2)]
        arrays += [swap(x, dc=1) for x in arrays]
        last = step == STEPS - 1
        mine = kept = call(
            functools.partial(
                outer_kernel, (l1, p_dev, pop, kblk, cond), len(arrays)
            ),
            shape((cond, width), jnp.float32 if last else jnp.bfloat16),
            [counts, slots, long_w, inner, drive] + arrays,
            [VMEM] * (5 + len(arrays)),
            2 * cond * width * kblk * pop,
            scratch=[
                pltpu.VMEM((len(arrays) * l1 * p_dev, cond, pop), jnp.bfloat16)
            ],
        )
    return mine


def solution(mesh):
    in_specs = (
        P(None, AXES),
        P(None, AXES),
        P(AXES, None),
        P(AXES, None, None, None),
        P(AXES, None),
        P(),
        P(),
    )
    return jax.shard_map(
        body, mesh=mesh, in_specs=in_specs, out_specs=P(None, AXES), check_vma=False
    )
```

```python
import functools

import jax
import jax.numpy as jnp
from jax import lax
from jax.experimental import pallas as pl
from jax.experimental.pallas import tpu as pltpu
from jax.sharding import PartitionSpec as P

STEPS = 2
PIECES = 4
CORES = 2
AXES = ("area", "local")
VMEM = pl.BlockSpec(memory_space=pltpu.VMEM)
HBM = pl.BlockSpec(memory_space=pltpu.HBM)
DIMS = (((1,), (1,)), ((), ()))


def call(kernel, out, operands, in_specs, flops, scratch=(), out_specs=VMEM, aliases={}):
    moved = sum(x.size * x.dtype.itemsize for x in operands)
    return pl.pallas_call(
        kernel,
        out_shape=out,
        in_specs=in_specs,
        out_specs=out_specs,
        scratch_shapes=scratch,
        input_output_aliases=aliases,
        compiler_params=pltpu.CompilerParams(vmem_limit_bytes=24 * 2**20),
        cost_estimate=pl.CostEstimate(
            flops=flops, bytes_accessed=moved, transcendentals=0
        ),
    )(*operands)


def in_hbm(x):
    return pltpu.with_memory_space_constraint(x, pltpu.HBM)


def log2(n):
    bits = n.bit_length() - 1
    assert n == 1 << bits
    return bits


def pieces(a, b, n, sems):
    rows = a.shape[0] // n
    parts = [pl.ds(i * rows, rows) for i in range(n)]
    moves = [
        pltpu.make_async_copy(a.at[at], b.at[at], sems.at[i])
        for i, at in enumerate(parts)
    ]
    for move in moves:
        move.start()
    return moves


def within_kernel(x_ref, w_ref, out_ref, again_ref, sems):
    moves = pieces(w_ref, out_ref, PIECES, sems)
    again_ref[...] = x_ref[...]
    for move in moves:
        move.wait()


def long_kernel(sizes, *refs):
    nx, l1, l2, p_dev = sizes
    x_ref, columns_hbm, map_hbm, w_hbm, drive_hbm = refs[:5]
    w_ref, drive_ref, slots_ref, again_ref = refs[5:9]
    columns_ref, map_ref, wide_ref, sems, w_sems = refs[9:]
    moves = [
        pltpu.make_async_copy(a, b, sems.at[n])
        for n, (a, b) in enumerate(
            ((columns_hbm, columns_ref), (map_hbm, map_ref), (drive_hbm, drive_ref))
        )
    ]
    for move in moves:
        move.start()
    w_moves = pieces(w_hbm, wide_ref, p_dev, w_sems)
    again_ref[...] = x_ref[...]
    for move in moves:
        move.wait()
    area, local = lax.axis_index("area"), lax.axis_index("local")
    inside_bits = log2(l1 * l2 * p_dev)
    columns = columns_ref[...]
    logical = columns >> inside_bits
    inside = columns & ((1 << inside_bits) - 1)
    target = jnp.zeros_like(columns)
    for a in range(nx * CORES):
        target = jnp.where(logical == a, map_ref[a], target)
    da = target ^ area
    dl = (inside >> log2(p_dev)) ^ local
    n = (da & (CORES - 1)) * nx + (da >> log2(CORES))
    n = n * l2 + (dl & (l2 - 1))
    n = n * l1 + (dl >> log2(l2))
    slots_ref[...] = n * p_dev + (inside & (p_dev - 1))
    for p, move in enumerate(w_moves):
        move.wait()
        for k in range(w_ref.shape[1]):
            w_ref[p, k] = wide_ref[p, k].T


def count_of(counts_ref):
    count = counts_ref[0]
    for a in range(1, counts_ref.shape[0]):
        count = jnp.where(lax.axis_index("area") == a, counts_ref[a], count)
    return count


def column_kernel(l2, p_dev, pop, order, counts_ref, *refs):
    out_ref = refs[-1]
    cond = refs[0].shape[0]
    count = count_of(counts_ref)
    for d, block in zip(order, refs[:-1]):
        first = (lax.axis_index("local") ^ (d * l2)) * p_dev
        for s in range(p_dev):
            at = slice(s * pop, (s + 1) * pop)
            x = block[:, at]
            out_ref[d * cond : (d + 1) * cond, at] = jnp.where(
                first + s < count, x, jnp.zeros_like(x)
            )


def lay(arrays, table, start, cond):
    pop = table.shape[2]
    at = start
    for a in arrays:
        for d in range(a.shape[0] // cond):
            for s in range(a.shape[1] // pop):
                table[at] = a[d * cond : (d + 1) * cond, s * pop : (s + 1) * pop]
                at += 1


def inner_kernel(l2, other, cond, *refs):
    blocks_ref, w_ref = refs[:2]
    here = lax.axis_index("local")
    width = blocks_ref.shape[1]
    total = None
    if not other:
        out_ref, again_ref = refs[2:]
        again_ref[...] = blocks_ref[...]
    elif len(refs) == 4:
        total, out_ref = refs[2][...], refs[3]
    else:
        total, arrays, out_ref, table = refs[2][...], refs[3:-2], refs[-2], refs[-1]
        lay(arrays, table, 0, cond)
    for d in range(blocks_ref.shape[0] // cond):
        l = here ^ (d * l2 + other)
        at = pl.ds(pl.multiple_of(l * width, width), width)
        part = lax.dot_general(
            blocks_ref[d * cond : (d + 1) * cond, :],
            w_ref[:, at],
            DIMS,
            preferred_element_type=jnp.float32,
        )
        total = part if total is None else total + part
    out_ref[...] = total


def outer_kernel(start, *refs):
    counts_ref, slots_ref, w_ref, inner_ref, drive_ref = refs[:5]
    arrays, out_ref, table = refs[5:-3], refs[-2], refs[-1]
    p_dev, kblk, pop, _ = w_ref.shape
    lay(arrays, table, start, out_ref.shape[0])
    count = count_of(counts_ref)
    first = lax.axis_index("local") * p_dev
    for p in range(p_dev):
        picked = jnp.concatenate([table[slots_ref[p, k]] for k in range(kblk)], axis=1)
        weights = w_ref[p].reshape(kblk * pop, pop)
        outer = jnp.dot(picked, weights, preferred_element_type=jnp.float32)
        here = slice(p * pop, (p + 1) * pop)
        rates = jnp.tanh(inner_ref[:, here] + outer + drive_ref[:, here])
        present = jnp.where(first + p < count, 1.0, 0.0)
        out_ref[:, here] = (rates * present).astype(out_ref.dtype)


def body(rates_init, drive, within_w, long_w, columns, area_map, counts):
    areas, locs = lax.axis_size("area"), lax.axis_size("local")
    nx, l1 = areas // CORES, 4
    l2 = locs // l1
    p_dev, kblk, pop, _ = long_w.shape
    cond, width = rates_init.shape
    devices = areas * locs

    def swap(x, dx=0, dc=0, d1=0, d2=0):
        by = (dx * CORES + dc) * locs + d1 * l2 + d2
        return lax.ppermute(x, AXES, [(i, i ^ by) for i in range(devices)])

    mine = rates_init.astype(jnp.bfloat16)
    shape = jax.ShapeDtypeStruct
    within_w, kept = call(
        within_kernel,
        [pltpu.VMEM(x.shape, x.dtype) for x in (within_w, mine)],
        [mine, in_hbm(within_w)],
        [VMEM, HBM],
        0,
        scratch=[pltpu.SemaphoreType.DMA((PIECES,))],
        out_specs=[VMEM] * 2,
    )
    for step in range(STEPS):
        order = (1, 3, 2)
        column = call(
            functools.partial(column_kernel, l2, p_dev, pop, (0,) + order),
            shape((l1 * cond, width), mine.dtype),
            [counts, kept] + [swap(mine, d1=d) for d in order],
            [VMEM] * (1 + l1),
            0,
        )
        got = {
            (dx, d2): swap(column, dx=dx, d2=d2) if dx or d2 else column
            for dx in range(nx)
            for d2 in range(l2)
        }
        if step == 0:
            long_w, drive, slots, got[0, 0] = call(
                functools.partial(long_kernel, (nx, l1, l2, p_dev)),
                [
                    pltpu.VMEM(x.shape, x.dtype)
                    for x in (long_w, drive, columns, column)
                ],
                [column] + [in_hbm(x) for x in (columns, area_map, long_w, drive)],
                [VMEM] + [HBM] * 4,
                0,
                scratch=[
                    pltpu.VMEM(columns.shape, columns.dtype),
                    pltpu.VMEM(area_map.shape, area_map.dtype),
                    pltpu.VMEM(long_w.shape, long_w.dtype),
                    pltpu.SemaphoreType.DMA((3,)),
                    pltpu.SemaphoreType.DMA((p_dev,)),
                ],
                out_specs=[VMEM] * 4,
            )
        partial = shape((cond, width), jnp.float32)
        flops = 2 * cond * width * width * l1
        inner, got[0, 0] = call(
            functools.partial(inner_kernel, l2, 0, cond),
            [partial, shape(column.shape, column.dtype)],
            (got[0, 0], within_w),
            [VMEM] * 2,
            flops,
            out_specs=[VMEM] * 2,
        )
        for d2 in range(1, l2 - 1):
            inner = call(
                functools.partial(inner_kernel, l2, d2, cond),
                partial,
                (got[0, d2], within_w, inner),
                [VMEM] * 3,
                flops,
            )
        arrays = [got[dx, d2] for dx in range(nx) for d2 in range(l2)]
        arrays += [swap(x, dc=1) for x in arrays]
        early = len(arrays) // 2 + 1
        per = l1 * p_dev
        table = pltpu.VMEM((len(arrays) * per, cond, pop), mine.dtype)
        inner, picks = call(
            functools.partial(inner_kernel, l2, l2 - 1, cond),
            [partial, table],
            [got[0, l2 - 1], within_w, inner] + arrays[:early],
            [VMEM] * (3 + early),
            flops,
            out_specs=[VMEM] * 2,
        )
        operands = [counts, slots, long_w, inner, drive] + arrays[early:] + [picks]
        last = step == STEPS - 1
        mine, _ = call(
            functools.partial(outer_kernel, early * per),
            [shape((cond, width), jnp.float32 if last else jnp.bfloat16), table],
            operands,
            [VMEM] * len(operands),
            2 * cond * width * kblk * pop,
            out_specs=[VMEM] * 2,
            aliases={len(operands) - 1: 1},
        )
        kept = mine
    return mine


def solution(mesh):
    in_specs = (
        P(None, AXES),
        P(None, AXES),
        P(AXES, None),
        P(AXES, None, None, None),
        P(AXES, None),
        P(),
        P(),
    )
    return jax.shard_map(
        body, mesh=mesh, in_specs=in_specs, out_specs=P(None, AXES), check_vma=False
    )
```

```python
import functools

import jax
import jax.numpy as jnp
from jax import lax
from jax.experimental import pallas as pl
from jax.experimental.pallas import tpu as pltpu
from jax.sharding import PartitionSpec as P

STEPS = 2
PIECES = 4
CORES = 2
AXES = ("area", "local")
VMEM = pl.BlockSpec(memory_space=pltpu.VMEM)
HBM = pl.BlockSpec(memory_space=pltpu.HBM)
DIMS = (((1,), (1,)), ((), ()))


def call(kernel, out, operands, in_specs, flops, scratch=(), out_specs=VMEM, aliases={}):
    moved = sum(x.size * x.dtype.itemsize for x in operands)
    return pl.pallas_call(
        kernel,
        out_shape=out,
        in_specs=in_specs,
        out_specs=out_specs,
        scratch_shapes=scratch,
        input_output_aliases=aliases,
        compiler_params=pltpu.CompilerParams(vmem_limit_bytes=24 * 2**20),
        cost_estimate=pl.CostEstimate(
            flops=flops, bytes_accessed=moved, transcendentals=0
        ),
    )(*operands)


def in_hbm(x):
    return pltpu.with_memory_space_constraint(x, pltpu.HBM)


def log2(n):
    bits = n.bit_length() - 1
    assert n == 1 << bits
    return bits


def pieces(a, b, n, sems):
    rows = a.shape[0] // n
    parts = [pl.ds(i * rows, rows) for i in range(n)]
    moves = [
        pltpu.make_async_copy(a.at[at], b.at[at], sems.at[i])
        for i, at in enumerate(parts)
    ]
    for move in moves:
        move.start()
    return moves


def within_kernel(x_ref, w_ref, out_ref, again_ref, sems):
    moves = pieces(w_ref, out_ref, PIECES, sems)
    again_ref[...] = x_ref[...]
    for move in moves:
        move.wait()


def long_kernel(sizes, *refs):
    nx, l1, l2, p_dev = sizes
    x_ref, columns_hbm, map_hbm, w_hbm, drive_hbm = refs[:5]
    w_ref, drive_ref, slots_ref, again_ref = refs[5:9]
    columns_ref, map_ref, wide_ref, sems, w_sems = refs[9:]
    moves = [
        pltpu.make_async_copy(a, b, sems.at[n])
        for n, (a, b) in enumerate(
            ((columns_hbm, columns_ref), (map_hbm, map_ref), (drive_hbm, drive_ref))
        )
    ]
    for move in moves:
        move.start()
    w_moves = pieces(w_hbm, wide_ref, p_dev, w_sems)
    again_ref[...] = x_ref[...]
    for move in moves:
        move.wait()
    area, local = lax.axis_index("area"), lax.axis_index("local")
    inside_bits = log2(l1 * l2 * p_dev)
    columns = columns_ref[...]
    logical = columns >> inside_bits
    inside = columns & ((1 << inside_bits) - 1)
    target = jnp.zeros_like(columns)
    for a in range(nx * CORES):
        target = jnp.where(logical == a, map_ref[a], target)
    da = target ^ area
    dl = (inside >> log2(p_dev)) ^ local
    n = (da & (CORES - 1)) * nx + (da >> log2(CORES))
    n = n * l2 + (dl & (l2 - 1))
    n = n * l1 + (dl >> log2(l2))
    slots_ref[...] = n * p_dev + (inside & (p_dev - 1))
    for p, move in enumerate(w_moves):
        move.wait()
        for k in range(w_ref.shape[1]):
            w_ref[p, k] = wide_ref[p, k].T


def count_of(counts_ref):
    count = counts_ref[0]
    for a in range(1, counts_ref.shape[0]):
        count = jnp.where(lax.axis_index("area") == a, counts_ref[a], count)
    return count


def column_kernel(l2, p_dev, pop, order, masked, counts_ref, *refs):
    out_ref = refs[-1]
    cond = refs[0].shape[0]
    count = count_of(counts_ref)
    for d, block in zip(order, refs[:-1]):
        if not masked:
            out_ref[d * cond : (d + 1) * cond, :] = block[...]
            continue
        first = (lax.axis_index("local") ^ (d * l2)) * p_dev
        for s in range(p_dev):
            at = slice(s * pop, (s + 1) * pop)
            x = block[:, at]
            out_ref[d * cond : (d + 1) * cond, at] = jnp.where(
                first + s < count, x, jnp.zeros_like(x)
            )


def lay(arrays, table, start, cond):
    pop = table.shape[2]
    at = start
    for a in arrays:
        for d in range(a.shape[0] // cond):
            for s in range(a.shape[1] // pop):
                table[at] = a[d * cond : (d + 1) * cond, s * pop : (s + 1) * pop]
                at += 1


def inner_kernel(l2, other, cond, *refs):
    blocks_ref, w_ref = refs[:2]
    here = lax.axis_index("local")
    width = blocks_ref.shape[1]
    total = None
    if not other:
        out_ref, again_ref = refs[2:]
        again_ref[...] = blocks_ref[...]
    elif len(refs) == 4:
        total, out_ref = refs[2][...], refs[3]
    else:
        total, arrays, out_ref, table = refs[2][...], refs[3:-2], refs[-2], refs[-1]
        lay(arrays, table, 0, cond)
    for d in range(blocks_ref.shape[0] // cond):
        l = here ^ (d * l2 + other)
        at = pl.ds(pl.multiple_of(l * width, width), width)
        part = lax.dot_general(
            blocks_ref[d * cond : (d + 1) * cond, :],
            w_ref[:, at],
            DIMS,
            preferred_element_type=jnp.float32,
        )
        total = part if total is None else total + part
    out_ref[...] = total


def outer_kernel(start, *refs):
    counts_ref, slots_ref, w_ref, inner_ref, drive_ref = refs[:5]
    arrays, out_ref, table = refs[5:-3], refs[-2], refs[-1]
    p_dev, kblk, pop, _ = w_ref.shape
    lay(arrays, table, start, out_ref.shape[0])
    count = count_of(counts_ref)
    first = lax.axis_index("local") * p_dev
    for p in range(p_dev):
        picked = jnp.concatenate([table[slots_ref[p, k]] for k in range(kblk)], axis=1)
        weights = w_ref[p].reshape(kblk * pop, pop)
        outer = jnp.dot(picked, weights, preferred_element_type=jnp.float32)
        here = slice(p * pop, (p + 1) * pop)
        rates = jnp.tanh(inner_ref[:, here] + outer + drive_ref[:, here])
        present = jnp.where(first + p < count, 1.0, 0.0)
        out_ref[:, here] = (rates * present).astype(out_ref.dtype)


def body(rates_init, drive, within_w, long_w, columns, area_map, counts):
    areas, locs = lax.axis_size("area"), lax.axis_size("local")
    nx, l1 = areas // CORES, 4
    l2 = locs // l1
    p_dev, kblk, pop, _ = long_w.shape
    cond, width = rates_init.shape
    devices = areas * locs

    def swap(x, dx=0, dc=0, d1=0, d2=0):
        by = (dx * CORES + dc) * locs + d1 * l2 + d2
        return lax.ppermute(x, AXES, [(i, i ^ by) for i in range(devices)])

    mine = rates_init.astype(jnp.bfloat16)
    shape = jax.ShapeDtypeStruct
    within_w, kept = call(
        within_kernel,
        [pltpu.VMEM(x.shape, x.dtype) for x in (within_w, mine)],
        [mine, in_hbm(within_w)],
        [VMEM, HBM],
        0,
        scratch=[pltpu.SemaphoreType.DMA((PIECES,))],
        out_specs=[VMEM] * 2,
    )
    for step in range(STEPS):
        order = (1, 3, 2)
        column = call(
            functools.partial(column_kernel, l2, p_dev, pop, (0,) + order, step == 0),
            shape((l1 * cond, width), mine.dtype),
            [counts, kept] + [swap(mine, d1=d) for d in order],
            [VMEM] * (1 + l1),
            0,
        )
        got = {
            (dx, d2): swap(column, dx=dx, d2=d2) if dx or d2 else column
            for dx in range(nx)
            for d2 in range(l2)
        }
        if step == 0:
            long_w, drive, slots, got[0, 0] = call(
                functools.partial(long_kernel, (nx, l1, l2, p_dev)),
                [
                    pltpu.VMEM(x.shape, x.dtype)
                    for x in (long_w, drive, columns, column)
                ],
                [column] + [in_hbm(x) for x in (columns, area_map, long_w, drive)],
                [VMEM] + [HBM] * 4,
                0,
                scratch=[
                    pltpu.VMEM(columns.shape, columns.dtype),
                    pltpu.VMEM(area_map.shape, area_map.dtype),
                    pltpu.VMEM(long_w.shape, long_w.dtype),
                    pltpu.SemaphoreType.DMA((3,)),
                    pltpu.SemaphoreType.DMA((p_dev,)),
                ],
                out_specs=[VMEM] * 4,
            )
        partial = shape((cond, width), jnp.float32)
        flops = 2 * cond * width * width * l1
        inner, got[0, 0] = call(
            functools.partial(inner_kernel, l2, 0, cond),
            [partial, shape(column.shape, column.dtype)],
            (got[0, 0], within_w),
            [VMEM] * 2,
            flops,
            out_specs=[VMEM] * 2,
        )
        for d2 in range(1, l2 - 1):
            inner = call(
                functools.partial(inner_kernel, l2, d2, cond),
                partial,
                (got[0, d2], within_w, inner),
                [VMEM] * 3,
                flops,
            )
        arrays = [got[dx, d2] for dx in range(nx) for d2 in range(l2)]
        arrays += [swap(x, dc=1) for x in arrays]
        early = len(arrays) // 2 + 1
        per = l1 * p_dev
        table = pltpu.VMEM((len(arrays) * per, cond, pop), mine.dtype)
        inner, picks = call(
            functools.partial(inner_kernel, l2, l2 - 1, cond),
            [partial, table],
            [got[0, l2 - 1], within_w, inner] + arrays[:early],
            [VMEM] * (3 + early),
            flops,
            out_specs=[VMEM] * 2,
        )
        operands = [counts, slots, long_w, inner, drive] + arrays[early:] + [picks]
        last = step == STEPS - 1
        mine, _ = call(
            functools.partial(outer_kernel, early * per),
            [shape((cond, width), jnp.float32 if last else jnp.bfloat16), table],
            operands,
            [VMEM] * len(operands),
            2 * cond * width * kblk * pop,
            out_specs=[VMEM] * 2,
            aliases={len(operands) - 1: 1},
        )
        kept = mine
    return mine


def solution(mesh):
    in_specs = (
        P(None, AXES),
        P(None, AXES),
        P(AXES, None),
        P(AXES, None, None, None),
        P(AXES, None),
        P(),
        P(),
    )
    return jax.shard_map(
        body, mesh=mesh, in_specs=in_specs, out_specs=P(None, AXES), check_vma=False
    )
```

```python
import functools

import jax
import jax.numpy as jnp
from jax import lax
from jax.experimental import pallas as pl
from jax.experimental.pallas import tpu as pltpu
from jax.sharding import PartitionSpec as P

STEPS = 2
PIECES = 4
FIRST = ((0, 0), (1, 1), (3, 2), (2, 3))
SECOND = ((0, 0), (1, 1), (2, 3), (3, 2))
CORES = 2
AXES = ("area", "local")
VMEM = pl.BlockSpec(memory_space=pltpu.VMEM)
HBM = pl.BlockSpec(memory_space=pltpu.HBM)
DIMS = (((1,), (1,)), ((), ()))


def call(kernel, out, operands, in_specs, flops, scratch=(), out_specs=VMEM, aliases={}):
    moved = sum(x.size * x.dtype.itemsize for x in operands)
    return pl.pallas_call(
        kernel,
        out_shape=out,
        in_specs=in_specs,
        out_specs=out_specs,
        scratch_shapes=scratch,
        input_output_aliases=aliases,
        compiler_params=pltpu.CompilerParams(vmem_limit_bytes=24 * 2**20),
        cost_estimate=pl.CostEstimate(
            flops=flops, bytes_accessed=moved, transcendentals=0
        ),
    )(*operands)


def in_hbm(x):
    return pltpu.with_memory_space_constraint(x, pltpu.HBM)


def log2(n):
    bits = n.bit_length() - 1
    assert n == 1 << bits
    return bits


def pieces(a, b, n, sems):
    rows = a.shape[0] // n
    parts = [pl.ds(i * rows, rows) for i in range(n)]
    moves = [
        pltpu.make_async_copy(a.at[at], b.at[at], sems.at[i])
        for i, at in enumerate(parts)
    ]
    for move in moves:
        move.start()
    return moves


def within_kernel(x_ref, w_ref, out_ref, again_ref, sems):
    moves = pieces(w_ref, out_ref, PIECES, sems)
    again_ref[...] = x_ref[...]
    for move in moves:
        move.wait()


def long_kernel(p_area, places, *refs):
    x_ref, columns_hbm, map_hbm, w_hbm, drive_hbm = refs[:5]
    w_ref, drive_ref, slots_ref, again_ref = refs[5:9]
    columns_ref, map_ref, wide_ref, sems, w_sems = refs[9:]
    p_dev = w_ref.shape[0]
    moves = [
        pltpu.make_async_copy(a, b, sems.at[n])
        for n, (a, b) in enumerate(
            ((columns_hbm, columns_ref), (map_hbm, map_ref), (drive_hbm, drive_ref))
        )
    ]
    for move in moves:
        move.start()
    w_moves = pieces(w_hbm, wide_ref, p_dev, w_sems)
    again_ref[...] = x_ref[...]
    for move in moves:
        move.wait()
    area, local = lax.axis_index("area"), lax.axis_index("local")
    inside_bits = log2(p_area)
    columns = columns_ref[...]
    logical = columns >> inside_bits
    inside = columns & ((1 << inside_bits) - 1)
    target = jnp.zeros_like(columns)
    for a in range(map_ref.shape[0]):
        target = jnp.where(logical == a, map_ref[a], target)
    da = target ^ area
    dl = (inside >> log2(p_dev)) ^ local
    dc = da & (CORES - 1)
    away = (da >> log2(CORES)) * (p_area // p_dev) + dl
    place = jnp.zeros_like(columns)
    for core in range(CORES):
        held = ((target & (CORES - 1)) == core).astype(jnp.int32)
        for by, at in places[core].items():
            place = jnp.where((away == by) & (held == 1), at, place)
    place = dc * len(places[0]) + place
    slots_ref[...] = place * p_dev + (inside & (p_dev - 1))
    for p, move in enumerate(w_moves):
        move.wait()
        for k in range(w_ref.shape[1]):
            w_ref[p, k] = wide_ref[p, k].T


def count_of(counts_ref, area):
    count = counts_ref[0]
    for a in range(1, counts_ref.shape[0]):
        count = jnp.where(area == a, counts_ref[a], count)
    return count


def column_kernel(parts, p_dev, pop, counts_ref, *refs):
    out_ref = refs[-1]
    cond = refs[0].shape[0]
    area, local = lax.axis_index("area"), lax.axis_index("local")
    for (d, far), block in zip(parts, refs[:-1]):
        if far is None:
            out_ref[d * cond : (d + 1) * cond, :] = block[...]
            continue
        (x0, l0), (x1, l1) = far
        odd = area & 1
        count = count_of(counts_ref, area ^ (jnp.where(odd == 1, x1, x0) * CORES))
        first = (local ^ jnp.where(odd == 1, l1, l0)) * p_dev
        for s in range(p_dev):
            at = slice(s * pop, (s + 1) * pop)
            x = block[:, at]
            out_ref[d * cond : (d + 1) * cond, at] = jnp.where(
                first + s < count, x, jnp.zeros_like(x)
            )


def lay(arrays, table, start, cond):
    pop = table.shape[2]
    at = start
    for a in arrays:
        for d in range(a.shape[0] // cond):
            for s in range(a.shape[1] // pop):
                table[at] = a[d * cond : (d + 1) * cond, s * pop : (s + 1) * pop]
                at += 1


def add_inner(lists, cond, arrays, w_ref, start_ref, out_ref):
    here = lax.axis_index("local")
    width = out_ref.shape[1]

    def add(blocks):
        total = None if start_ref is None else start_ref[...]
        for n, d, far in blocks:
            at = pl.ds(pl.multiple_of((here ^ far) * width, width), width)
            part = lax.dot_general(
                arrays[n][d * cond : (d + 1) * cond, :],
                w_ref[:, at],
                DIMS,
                preferred_element_type=jnp.float32,
            )
            total = part if total is None else total + part
        out_ref[...] = total

    if lists[0] == lists[1]:
        add(lists[0])
        return
    odd = lax.axis_index("area") & 1
    for core in range(CORES):
        pl.when(odd == core)(functools.partial(add, lists[core]))


def inner_kernel(lists, cond, blocks_ref, w_ref, out_ref, again_ref):
    again_ref[...] = blocks_ref[...]
    add_inner(lists, cond, [blocks_ref], w_ref, None, out_ref)


def rest_kernel(lists, cond, w_ref, start_ref, *refs):
    arrays, out_ref, table = refs[:-2], refs[-2], refs[-1]
    lay(arrays, table, 0, cond)
    add_inner(lists, cond, arrays, w_ref, start_ref, out_ref)


def outer_kernel(start, *refs):
    counts_ref, slots_ref, w_ref, inner_ref, drive_ref = refs[:5]
    arrays, out_ref, table = refs[5:-3], refs[-2], refs[-1]
    p_dev, kblk, pop, _ = w_ref.shape
    lay(arrays, table, start, out_ref.shape[0])
    count = count_of(counts_ref, lax.axis_index("area"))
    first = lax.axis_index("local") * p_dev
    for p in range(p_dev):
        picked = jnp.concatenate([table[slots_ref[p, k]] for k in range(kblk)], axis=1)
        weights = w_ref[p].reshape(kblk * pop, pop)
        outer = jnp.dot(picked, weights, preferred_element_type=jnp.float32)
        here = slice(p * pop, (p + 1) * pop)
        rates = jnp.tanh(inner_ref[:, here] + outer + drive_ref[:, here])
        present = jnp.where(first + p < count, 1.0, 0.0)
        out_ref[:, here] = (rates * present).astype(out_ref.dtype)


def plan(nx, l1, l2):
    line = [(0, d * l2) for d in range(l1)]
    plane = [(dx, d2) for dx in range(nx) for d2 in range(l2)]
    if len(line) != len(plane):
        return [(a, a) for a in line], [(a, a) for a in plane]
    first = [(line[a], plane[b]) for a, b in FIRST]
    second = [(plane[a], line[b]) for a, b in SECOND]
    return first, second


def body(rates_init, drive, within_w, long_w, columns, area_map, counts):
    areas, locs = lax.axis_size("area"), lax.axis_size("local")
    nx, l1 = areas // CORES, 4
    l2 = locs // l1
    p_dev, kblk, pop, _ = long_w.shape
    cond, width = rates_init.shape
    devices = areas * locs
    first, second = plan(nx, l1, l2)
    places = [{}, {}]
    lists = [([], []), ([], [])]
    for core in range(CORES):
        for n, by_n in enumerate(second):
            for d, by_d in enumerate(first):
                dx = by_n[core][0] ^ by_d[core][0]
                dl = by_n[core][1] ^ by_d[core][1]
                places[core][dx * locs + dl] = n * len(first) + d
                if dx == 0:
                    lists[n > 0][core].append((n, d, dl))

    def swap(x, by):
        far = [dx * CORES * locs + dl for dx, dl in by]
        return lax.ppermute(
            x, AXES, [(i, i ^ far[(i // locs) % CORES]) for i in range(devices)]
        )

    def across(x):
        return lax.ppermute(x, AXES, [(i, i ^ locs) for i in range(devices)])

    mine = rates_init.astype(jnp.bfloat16)
    shape = jax.ShapeDtypeStruct
    within_w, kept = call(
        within_kernel,
        [pltpu.VMEM(x.shape, x.dtype) for x in (within_w, mine)],
        [mine, in_hbm(within_w)],
        [VMEM, HBM],
        0,
        scratch=[pltpu.SemaphoreType.DMA((PIECES,))],
        out_specs=[VMEM] * 2,
    )
    for step in range(STEPS):
        column = call(
            functools.partial(
                column_kernel,
                [(d, None if step else by) for d, by in enumerate(first)],
                p_dev,
                pop,
            ),
            shape((len(first) * cond, width), mine.dtype),
            [counts, kept] + [swap(mine, by) for by in first[1:]],
            [VMEM] * (1 + len(first)),
            0,
        )
        whole = column
        if step == 0:
            long_w, drive, slots, whole = call(
                functools.partial(long_kernel, locs * p_dev, places),
                [
                    pltpu.VMEM(x.shape, x.dtype)
                    for x in (long_w, drive, columns, column)
                ],
                [column] + [in_hbm(x) for x in (columns, area_map, long_w, drive)],
                [VMEM] + [HBM] * 4,
                0,
                scratch=[
                    pltpu.VMEM(columns.shape, columns.dtype),
                    pltpu.VMEM(area_map.shape, area_map.dtype),
                    pltpu.VMEM(long_w.shape, long_w.dtype),
                    pltpu.SemaphoreType.DMA((3,)),
                    pltpu.SemaphoreType.DMA((p_dev,)),
                ],
                out_specs=[VMEM] * 4,
            )
        partial = shape((cond, width), jnp.float32)
        flops = 2 * cond * width * width * l1
        inner, whole = call(
            functools.partial(inner_kernel, lists[0], cond),
            [partial, shape(column.shape, column.dtype)],
            (whole, within_w),
            [VMEM] * 2,
            flops,
            out_specs=[VMEM] * 2,
        )
        arrays = [whole] + [swap(column, by) for by in second[1:]]
        arrays += [across(x) for x in arrays]
        early = len(second) + 1
        per = len(first) * p_dev
        table = pltpu.VMEM((len(arrays) * per, cond, pop), mine.dtype)
        inner, picks = call(
            functools.partial(rest_kernel, lists[1], cond),
            [partial, table],
            [within_w, inner] + arrays[:early],
            [VMEM] * (2 + early),
            flops,
            out_specs=[VMEM] * 2,
        )
        operands = [counts, slots, long_w, inner, drive] + arrays[early:] + [picks]
        last = step == STEPS - 1
        mine, _ = call(
            functools.partial(outer_kernel, early * per),
            [shape((cond, width), jnp.float32 if last else jnp.bfloat16), table],
            operands,
            [VMEM] * len(operands),
            2 * cond * width * kblk * pop,
            out_specs=[VMEM] * 2,
            aliases={len(operands) - 1: 1},
        )
        kept = mine
    return mine


def solution(mesh):
    in_specs = (
        P(None, AXES),
        P(None, AXES),
        P(AXES, None),
        P(AXES, None, None, None),
        P(AXES, None),
        P(),
        P(),
    )
    return jax.shard_map(
        body, mesh=mesh, in_specs=in_specs, out_specs=P(None, AXES), check_vma=False
    )
```

```python
import functools

import jax
import jax.numpy as jnp
from jax import lax
from jax.experimental import pallas as pl
from jax.experimental.pallas import tpu as pltpu
from jax.sharding import PartitionSpec as P

STEPS = 2
PIECES = 4
FIRST = ((0, 0), (1, 1), (3, 2), (2, 3))
SECOND = ((0, 0), (1, 1), (2, 3), (3, 2))
CORES = 2
AXES = ("area", "local")
VMEM = pl.BlockSpec(memory_space=pltpu.VMEM)
HBM = pl.BlockSpec(memory_space=pltpu.HBM)
DIMS = (((1,), (1,)), ((), ()))


def call(kernel, out, operands, in_specs, flops, scratch=(), out_specs=VMEM, aliases={}):
    moved = sum(x.size * x.dtype.itemsize for x in operands)
    return pl.pallas_call(
        kernel,
        out_shape=out,
        in_specs=in_specs,
        out_specs=out_specs,
        scratch_shapes=scratch,
        input_output_aliases=aliases,
        compiler_params=pltpu.CompilerParams(vmem_limit_bytes=24 * 2**20),
        cost_estimate=pl.CostEstimate(
            flops=flops, bytes_accessed=moved, transcendentals=0
        ),
    )(*operands)


def in_hbm(x):
    return pltpu.with_memory_space_constraint(x, pltpu.HBM)


def log2(n):
    bits = n.bit_length() - 1
    assert n == 1 << bits
    return bits


def pieces(a, b, n, sems):
    rows = a.shape[0] // n
    parts = [pl.ds(i * rows, rows) for i in range(n)]
    moves = [
        pltpu.make_async_copy(a.at[at], b.at[at], sems.at[i])
        for i, at in enumerate(parts)
    ]
    for move in moves:
        move.start()
    return moves


def within_kernel(x_ref, w_ref, out_ref, again_ref, sems):
    moves = pieces(w_ref, out_ref, PIECES, sems)
    again_ref[...] = x_ref[...]
    for move in moves:
        move.wait()


def long_kernel(p_area, places, *refs):
    x_ref, columns_hbm, map_hbm, w_hbm, drive_hbm = refs[:5]
    w_ref, drive_ref, slots_ref, again_ref = refs[5:9]
    columns_ref, map_ref, wide_ref, sems, w_sems = refs[9:]
    p_dev = w_ref.shape[0]
    moves = [
        pltpu.make_async_copy(a, b, sems.at[n])
        for n, (a, b) in enumerate(
            ((columns_hbm, columns_ref), (map_hbm, map_ref), (drive_hbm, drive_ref))
        )
    ]
    for move in moves:
        move.start()
    again_ref[...] = x_ref[...]
    for p in range(p_dev):
        for k in range(w_ref.shape[1]):
            w_ref[p, k] = w_hbm[p, k].T
    for move in moves:
        move.wait()
    area, local = lax.axis_index("area"), lax.axis_index("local")
    inside_bits = log2(p_area)
    columns = columns_ref[...]
    logical = columns >> inside_bits
    inside = columns & ((1 << inside_bits) - 1)
    target = jnp.zeros_like(columns)
    for a in range(map_ref.shape[0]):
        target = jnp.where(logical == a, map_ref[a], target)
    da = target ^ area
    dl = (inside >> log2(p_dev)) ^ local
    dc = da & (CORES - 1)
    away = (da >> log2(CORES)) * (p_area // p_dev) + dl
    place = jnp.zeros_like(columns)
    for core in range(CORES):
        held = ((target & (CORES - 1)) == core).astype(jnp.int32)
        for by, at in places[core].items():
            place = jnp.where((away == by) & (held == 1), at, place)
    place = dc * len(places[0]) + place
    slots_ref[...] = place * p_dev + (inside & (p_dev - 1))


def count_of(counts_ref, area):
    count = counts_ref[0]
    for a in range(1, counts_ref.shape[0]):
        count = jnp.where(area == a, counts_ref[a], count)
    return count


def column_kernel(parts, p_dev, pop, counts_ref, *refs):
    out_ref = refs[-1]
    cond = refs[0].shape[0]
    area, local = lax.axis_index("area"), lax.axis_index("local")
    for (d, far), block in zip(parts, refs[:-1]):
        if far is None:
            out_ref[d * cond : (d + 1) * cond, :] = block[...]
            continue
        (x0, l0), (x1, l1) = far
        odd = area & 1
        count = count_of(counts_ref, area ^ (jnp.where(odd == 1, x1, x0) * CORES))
        first = (local ^ jnp.where(odd == 1, l1, l0)) * p_dev
        for s in range(p_dev):
            at = slice(s * pop, (s + 1) * pop)
            x = block[:, at]
            out_ref[d * cond : (d + 1) * cond, at] = jnp.where(
                first + s < count, x, jnp.zeros_like(x)
            )


def lay(arrays, table, start, cond):
    pop = table.shape[2]
    at = start
    for a in arrays:
        for d in range(a.shape[0] // cond):
            for s in range(a.shape[1] // pop):
                table[at] = a[d * cond : (d + 1) * cond, s * pop : (s + 1) * pop]
                at += 1


def add_inner(lists, cond, arrays, w_ref, start_ref, out_ref):
    here = lax.axis_index("local")
    width = out_ref.shape[1]

    def add(blocks):
        total = None if start_ref is None else start_ref[...]
        for n, d, far in blocks:
            at = pl.ds(pl.multiple_of((here ^ far) * width, width), width)
            part = lax.dot_general(
                arrays[n][d * cond : (d + 1) * cond, :],
                w_ref[:, at],
                DIMS,
                preferred_element_type=jnp.float32,
            )
            total = part if total is None else total + part
        out_ref[...] = total

    if lists[0] == lists[1]:
        add(lists[0])
        return
    odd = lax.axis_index("area") & 1
    for core in range(CORES):
        pl.when(odd == core)(functools.partial(add, lists[core]))


def inner_kernel(lists, cond, blocks_ref, w_ref, out_ref, again_ref):
    again_ref[...] = blocks_ref[...]
    add_inner(lists, cond, [blocks_ref], w_ref, None, out_ref)


def rest_kernel(lists, cond, w_ref, start_ref, *refs):
    arrays, out_ref, table = refs[:-2], refs[-2], refs[-1]
    lay(arrays, table, 0, cond)
    add_inner(lists, cond, arrays, w_ref, start_ref, out_ref)


def outer_kernel(start, *refs):
    counts_ref, slots_ref, w_ref, inner_ref, drive_ref = refs[:5]
    arrays, out_ref, table = refs[5:-3], refs[-2], refs[-1]
    p_dev, kblk, pop, _ = w_ref.shape
    lay(arrays, table, start, out_ref.shape[0])
    count = count_of(counts_ref, lax.axis_index("area"))
    first = lax.axis_index("local") * p_dev
    for p in range(p_dev):
        picked = jnp.concatenate([table[slots_ref[p, k]] for k in range(kblk)], axis=1)
        weights = w_ref[p].reshape(kblk * pop, pop)
        outer = jnp.dot(picked, weights, preferred_element_type=jnp.float32)
        here = slice(p * pop, (p + 1) * pop)
        rates = jnp.tanh(inner_ref[:, here] + outer + drive_ref[:, here])
        present = jnp.where(first + p < count, 1.0, 0.0)
        out_ref[:, here] = (rates * present).astype(out_ref.dtype)


def plan(nx, l1, l2):
    line = [(0, d * l2) for d in range(l1)]
    plane = [(dx, d2) for dx in range(nx) for d2 in range(l2)]
    if len(line) != len(plane):
        return [(a, a) for a in line], [(a, a) for a in plane]
    first = [(line[a], plane[b]) for a, b in FIRST]
    second = [(plane[a], line[b]) for a, b in SECOND]
    return first, second


def body(rates_init, drive, within_w, long_w, columns, area_map, counts):
    areas, locs = lax.axis_size("area"), lax.axis_size("local")
    nx, l1 = areas // CORES, 4
    l2 = locs // l1
    p_dev, kblk, pop, _ = long_w.shape
    cond, width = rates_init.shape
    devices = areas * locs
    first, second = plan(nx, l1, l2)
    places = [{}, {}]
    lists = [([], []), ([], [])]
    for core in range(CORES):
        for n, by_n in enumerate(second):
            for d, by_d in enumerate(first):
                dx = by_n[core][0] ^ by_d[core][0]
                dl = by_n[core][1] ^ by_d[core][1]
                places[core][dx * locs + dl] = n * len(first) + d
                if dx == 0:
                    lists[n > 0][core].append((n, d, dl))

    def swap(x, by):
        far = [dx * CORES * locs + dl for dx, dl in by]
        return lax.ppermute(
            x, AXES, [(i, i ^ far[(i // locs) % CORES]) for i in range(devices)]
        )

    def across(x):
        return lax.ppermute(x, AXES, [(i, i ^ locs) for i in range(devices)])

    mine = rates_init.astype(jnp.bfloat16)
    shape = jax.ShapeDtypeStruct
    within_w, kept = call(
        within_kernel,
        [pltpu.VMEM(x.shape, x.dtype) for x in (within_w, mine)],
        [mine, in_hbm(within_w)],
        [VMEM, HBM],
        0,
        scratch=[pltpu.SemaphoreType.DMA((PIECES,))],
        out_specs=[VMEM] * 2,
    )
    for step in range(STEPS):
        column = call(
            functools.partial(
                column_kernel,
                [(d, None if step else by) for d, by in enumerate(first)],
                p_dev,
                pop,
            ),
            shape((len(first) * cond, width), mine.dtype),
            [counts, kept] + [swap(mine, by) for by in first[1:]],
            [VMEM] * (1 + len(first)),
            0,
        )
        whole = column
        if step == 0:
            long_w, drive, slots, whole = call(
                functools.partial(long_kernel, locs * p_dev, places),
                [
                    pltpu.VMEM(x.shape, x.dtype)
                    for x in (long_w, drive, columns, column)
                ],
                [column, in_hbm(columns), in_hbm(area_map), long_w, in_hbm(drive)],
                [VMEM, HBM, HBM, VMEM, HBM],
                0,
                scratch=[
                    pltpu.VMEM(columns.shape, columns.dtype),
                    pltpu.VMEM(area_map.shape, area_map.dtype),
                    pltpu.VMEM(long_w.shape, long_w.dtype),
                    pltpu.SemaphoreType.DMA((3,)),
                    pltpu.SemaphoreType.DMA((p_dev,)),
                ],
                out_specs=[VMEM] * 4,
            )
        partial = shape((cond, width), jnp.float32)
        flops = 2 * cond * width * width * l1
        inner, whole = call(
            functools.partial(inner_kernel, lists[0], cond),
            [partial, shape(column.shape, column.dtype)],
            (whole, within_w),
            [VMEM] * 2,
            flops,
            out_specs=[VMEM] * 2,
        )
        arrays = [whole] + [swap(column, by) for by in second[1:]]
        arrays += [across(x) for x in arrays]
        early = len(second) + 1
        per = len(first) * p_dev
        table = pltpu.VMEM((len(arrays) * per, cond, pop), mine.dtype)
        inner, picks = call(
            functools.partial(rest_kernel, lists[1], cond),
            [partial, table],
            [within_w, inner] + arrays[:early],
            [VMEM] * (2 + early),
            flops,
            out_specs=[VMEM] * 2,
        )
        operands = [counts, slots, long_w, inner, drive] + arrays[early:] + [picks]
        last = step == STEPS - 1
        mine, _ = call(
            functools.partial(outer_kernel, early * per),
            [shape((cond, width), jnp.float32 if last else jnp.bfloat16), table],
            operands,
            [VMEM] * len(operands),
            2 * cond * width * kblk * pop,
            out_specs=[VMEM] * 2,
            aliases={len(operands) - 1: 1},
        )
        kept = mine
    return mine


def solution(mesh):
    in_specs = (
        P(None, AXES),
        P(None, AXES),
        P(AXES, None),
        P(AXES, None, None, None),
        P(AXES, None),
        P(),
        P(),
    )
    return jax.shard_map(
        body, mesh=mesh, in_specs=in_specs, out_specs=P(None, AXES), check_vma=False
    )
```

```python
import functools

import jax
import jax.numpy as jnp
from jax import lax
from jax.experimental import pallas as pl
from jax.experimental.pallas import tpu as pltpu
from jax.sharding import PartitionSpec as P

STEPS = 2
PIECES = 4
FIRST = ((0, 0), (1, 1), (3, 2), (2, 3))
SECOND = ((0, 0), (1, 1), (2, 3), (3, 2))
CORES = 2
AXES = ("area", "local")
VMEM = pl.BlockSpec(memory_space=pltpu.VMEM)
HBM = pl.BlockSpec(memory_space=pltpu.HBM)
DIMS = (((1,), (1,)), ((), ()))


def call(kernel, out, operands, in_specs, flops, scratch=(), out_specs=VMEM, aliases={}):
    moved = sum(x.size * x.dtype.itemsize for x in operands)
    return pl.pallas_call(
        kernel,
        out_shape=out,
        in_specs=in_specs,
        out_specs=out_specs,
        scratch_shapes=scratch,
        input_output_aliases=aliases,
        compiler_params=pltpu.CompilerParams(vmem_limit_bytes=24 * 2**20),
        cost_estimate=pl.CostEstimate(
            flops=flops, bytes_accessed=moved, transcendentals=0
        ),
    )(*operands)


def in_hbm(x):
    return pltpu.with_memory_space_constraint(x, pltpu.HBM)


def log2(n):
    bits = n.bit_length() - 1
    assert n == 1 << bits
    return bits


def pieces(a, b, n, sems):
    rows = a.shape[0] // n
    parts = [pl.ds(i * rows, rows) for i in range(n)]
    moves = [
        pltpu.make_async_copy(a.at[at], b.at[at], sems.at[i])
        for i, at in enumerate(parts)
    ]
    for move in moves:
        move.start()
    return moves


def within_kernel(x_ref, w_ref, out_ref, again_ref, sems):
    moves = pieces(w_ref, out_ref, PIECES, sems)
    again_ref[...] = x_ref[...]
    for move in moves:
        move.wait()


def long_kernel(p_area, places, *refs):
    x_ref, columns_hbm, map_hbm, w_hbm, drive_hbm = refs[:5]
    w_ref, drive_ref, slots_ref, again_ref = refs[5:9]
    columns_ref, map_ref, wide_ref, sems, w_sems = refs[9:]
    p_dev = w_ref.shape[0]
    moves = [
        pltpu.make_async_copy(a, b, sems.at[n])
        for n, (a, b) in enumerate(
            ((columns_hbm, columns_ref), (map_hbm, map_ref), (drive_hbm, drive_ref))
        )
    ]
    for move in moves:
        move.start()
    w_moves = pieces(w_hbm, wide_ref, p_dev, w_sems)
    again_ref[...] = x_ref[...]
    for p, move in enumerate(w_moves):
        move.wait()
        for k in range(w_ref.shape[1]):
            w_ref[p, k] = wide_ref[p, k].T
    for move in moves:
        move.wait()
    area, local = lax.axis_index("area"), lax.axis_index("local")
    inside_bits = log2(p_area)
    columns = columns_ref[...]
    logical = columns >> inside_bits
    inside = columns & ((1 << inside_bits) - 1)
    target = jnp.zeros_like(columns)
    for a in range(map_ref.shape[0]):
        target = jnp.where(logical == a, map_ref[a], target)
    da = target ^ area
    dl = (inside >> log2(p_dev)) ^ local
    dc = da & (CORES - 1)
    away = (da >> log2(CORES)) * (p_area // p_dev) + dl
    place = jnp.zeros_like(columns)
    for core in range(CORES):
        held = ((target & (CORES - 1)) == core).astype(jnp.int32)
        for by, at in places[core].items():
            place = jnp.where((away == by) & (held == 1), at, place)
    place = dc * len(places[0]) + place
    slots_ref[...] = place * p_dev + (inside & (p_dev - 1))


def count_of(counts_ref, area):
    count = counts_ref[0]
    for a in range(1, counts_ref.shape[0]):
        count = jnp.where(area == a, counts_ref[a], count)
    return count


def column_kernel(parts, p_dev, pop, counts_ref, *refs):
    out_ref = refs[-1]
    cond = refs[0].shape[0]
    area, local = lax.axis_index("area"), lax.axis_index("local")
    for (d, far), block in zip(parts, refs[:-1]):
        if far is None:
            out_ref[d * cond : (d + 1) * cond, :] = block[...]
            continue
        (x0, l0), (x1, l1) = far
        odd = area & 1
        count = count_of(counts_ref, area ^ (jnp.where(odd == 1, x1, x0) * CORES))
        first = (local ^ jnp.where(odd == 1, l1, l0)) * p_dev
        for s in range(p_dev):
            at = slice(s * pop, (s + 1) * pop)
            x = block[:, at]
            out_ref[d * cond : (d + 1) * cond, at] = jnp.where(
                first + s < count, x, jnp.zeros_like(x)
            )


def lay(arrays, table, start, cond):
    pop = table.shape[2]
    at = start
    for a in arrays:
        for d in range(a.shape[0] // cond):
            for s in range(a.shape[1] // pop):
                table[at] = a[d * cond : (d + 1) * cond, s * pop : (s + 1) * pop]
                at += 1


def add_inner(lists, cond, arrays, w_ref, start_ref, out_ref):
    here = lax.axis_index("local")
    width = out_ref.shape[1]

    def add(blocks):
        total = None if start_ref is None else start_ref[...]
        for n, d, far in blocks:
            at = pl.ds(pl.multiple_of((here ^ far) * width, width), width)
            part = lax.dot_general(
                arrays[n][d * cond : (d + 1) * cond, :],
                w_ref[:, at],
                DIMS,
                preferred_element_type=jnp.float32,
            )
            total = part if total is None else total + part
        out_ref[...] = total

    if lists[0] == lists[1]:
        add(lists[0])
        return
    odd = lax.axis_index("area") & 1
    for core in range(CORES):
        pl.when(odd == core)(functools.partial(add, lists[core]))


def inner_kernel(lists, cond, blocks_ref, w_ref, out_ref, again_ref):
    again_ref[...] = blocks_ref[...]
    add_inner(lists, cond, [blocks_ref], w_ref, None, out_ref)


def rest_kernel(lists, cond, w_ref, start_ref, *refs):
    arrays, out_ref, table = refs[:-2], refs[-2], refs[-1]
    lay(arrays, table, 0, cond)
    add_inner(lists, cond, arrays, w_ref, start_ref, out_ref)


def outer_kernel(start, *refs):
    counts_ref, slots_ref, w_ref, inner_ref, drive_ref = refs[:5]
    arrays, out_ref, table = refs[5:-3], refs[-2], refs[-1]
    p_dev, kblk, pop, _ = w_ref.shape
    lay(arrays, table, start, out_ref.shape[0])
    count = count_of(counts_ref, lax.axis_index("area"))
    first = lax.axis_index("local") * p_dev
    for p in range(p_dev):
        picked = jnp.concatenate([table[slots_ref[p, k]] for k in range(kblk)], axis=1)
        weights = w_ref[p].reshape(kblk * pop, pop)
        outer = jnp.dot(picked, weights, preferred_element_type=jnp.float32)
        here = slice(p * pop, (p + 1) * pop)
        rates = jnp.tanh(inner_ref[:, here] + outer + drive_ref[:, here])
        present = jnp.where(first + p < count, 1.0, 0.0)
        out_ref[:, here] = (rates * present).astype(out_ref.dtype)


def plan(nx, l1, l2):
    line = [(0, d * l2) for d in range(l1)]
    plane = [(dx, d2) for dx in range(nx) for d2 in range(l2)]
    if len(line) != len(plane):
        return [(a, a) for a in line], [(a, a) for a in plane]
    first = [(line[a], plane[b]) for a, b in FIRST]
    second = [(plane[a], line[b]) for a, b in SECOND]
    return first, second


def body(rates_init, drive, within_w, long_w, columns, area_map, counts):
    areas, locs = lax.axis_size("area"), lax.axis_size("local")
    nx, l1 = areas // CORES, 4
    l2 = locs // l1
    p_dev, kblk, pop, _ = long_w.shape
    cond, width = rates_init.shape
    devices = areas * locs
    first, second = plan(nx, l1, l2)
    places = [{}, {}]
    lists = [([], []), ([], [])]
    for core in range(CORES):
        for n, by_n in enumerate(second):
            for d, by_d in enumerate(first):
                dx = by_n[core][0] ^ by_d[core][0]
                dl = by_n[core][1] ^ by_d[core][1]
                places[core][dx * locs + dl] = n * len(first) + d
                if dx == 0:
                    lists[n > 0][core].append((n, d, dl))

    def swap(x, by):
        far = [dx * CORES * locs + dl for dx, dl in by]
        return lax.ppermute(
            x, AXES, [(i, i ^ far[(i // locs) % CORES]) for i in range(devices)]
        )

    def across(x):
        return lax.ppermute(x, AXES, [(i, i ^ locs) for i in range(devices)])

    mine = rates_init.astype(jnp.bfloat16)
    shape = jax.ShapeDtypeStruct
    within_w, kept = call(
        within_kernel,
        [pltpu.VMEM(x.shape, x.dtype) for x in (within_w, mine)],
        [mine, in_hbm(within_w)],
        [VMEM, HBM],
        0,
        scratch=[pltpu.SemaphoreType.DMA((PIECES,))],
        out_specs=[VMEM] * 2,
    )
    for step in range(STEPS):
        column = call(
            functools.partial(
                column_kernel,
                [(d, None if step else by) for d, by in enumerate(first)],
                p_dev,
                pop,
            ),
            shape((len(first) * cond, width), mine.dtype),
            [counts, kept] + [swap(mine, by) for by in first[1:]],
            [VMEM] * (1 + len(first)),
            0,
        )
        whole = column
        if step == 0:
            long_w, drive, slots, whole = call(
                functools.partial(long_kernel, locs * p_dev, places),
                [
                    pltpu.VMEM(x.shape, x.dtype)
                    for x in (long_w, drive, columns, column)
                ],
                [column] + [in_hbm(x) for x in (columns, area_map, long_w, drive)],
                [VMEM] + [HBM] * 4,
                0,
                scratch=[
                    pltpu.VMEM(columns.shape, columns.dtype),
                    pltpu.VMEM(area_map.shape, area_map.dtype),
                    pltpu.VMEM(long_w.shape, long_w.dtype),
                    pltpu.SemaphoreType.DMA((3,)),
                    pltpu.SemaphoreType.DMA((p_dev,)),
                ],
                out_specs=[VMEM] * 4,
            )
        partial = shape((cond, width), jnp.float32)
        flops = 2 * cond * width * width * l1
        inner, whole = call(
            functools.partial(inner_kernel, lists[0], cond),
            [partial, shape(column.shape, column.dtype)],
            (whole, within_w),
            [VMEM] * 2,
            flops,
            out_specs=[VMEM] * 2,
        )
        arrays = [whole] + [swap(column, by) for by in second[1:]]
        arrays += [across(x) for x in arrays]
        early = len(second) + 1
        per = len(first) * p_dev
        table = pltpu.VMEM((len(arrays) * per, cond, pop), mine.dtype)
        inner, picks = call(
            functools.partial(rest_kernel, lists[1], cond),
            [partial, table],
            [within_w, inner] + arrays[:early],
            [VMEM] * (2 + early),
            flops,
            out_specs=[VMEM] * 2,
        )
        operands = [counts, slots, long_w, inner, drive] + arrays[early:] + [picks]
        last = step == STEPS - 1
        mine, _ = call(
            functools.partial(outer_kernel, early * per),
            [shape((cond, width), jnp.float32 if last else jnp.bfloat16), table],
            operands,
            [VMEM] * len(operands),
            2 * cond * width * kblk * pop,
            out_specs=[VMEM] * 2,
            aliases={len(operands) - 1: 1},
        )
        kept = mine
    return mine


def solution(mesh):
    in_specs = (
        P(None, AXES),
        P(None, AXES),
        P(AXES, None),
        P(AXES, None, None, None),
        P(AXES, None),
        P(),
        P(),
    )
    return jax.shard_map(
        body, mesh=mesh, in_specs=in_specs, out_specs=P(None, AXES), check_vma=False
    )
```

```python
import functools

import jax
import jax.numpy as jnp
from jax import lax
from jax.experimental import pallas as pl
from jax.experimental.pallas import tpu as pltpu
from jax.sharding import PartitionSpec as P

STEPS = 2
PIECES = 4
FIRST = ((0, 0), (1, 1), (3, 2), (2, 3))
SECOND = ((0, 0), (1, 1), (2, 3), (3, 2))
CORES = 2
AXES = ("area", "local")
VMEM = pl.BlockSpec(memory_space=pltpu.VMEM)
HBM = pl.BlockSpec(memory_space=pltpu.HBM)
DIMS = (((1,), (1,)), ((), ()))


def call(kernel, out, operands, in_specs, flops, scratch=(), out_specs=VMEM, aliases={}):
    moved = sum(x.size * x.dtype.itemsize for x in operands)
    return pl.pallas_call(
        kernel,
        out_shape=out,
        in_specs=in_specs,
        out_specs=out_specs,
        scratch_shapes=scratch,
        input_output_aliases=aliases,
        compiler_params=pltpu.CompilerParams(vmem_limit_bytes=24 * 2**20),
        cost_estimate=pl.CostEstimate(
            flops=flops, bytes_accessed=moved, transcendentals=0
        ),
    )(*operands)


def in_hbm(x):
    return pltpu.with_memory_space_constraint(x, pltpu.HBM)


def log2(n):
    bits = n.bit_length() - 1
    assert n == 1 << bits
    return bits


def pieces(a, b, n, sems):
    rows = a.shape[0] // n
    parts = [pl.ds(i * rows, rows) for i in range(n)]
    moves = [
        pltpu.make_async_copy(a.at[at], b.at[at], sems.at[i])
        for i, at in enumerate(parts)
    ]
    for move in moves:
        move.start()
    return moves


def within_kernel(x_ref, w_ref, out_ref, again_ref, sems):
    moves = pieces(w_ref, out_ref, PIECES, sems)
    again_ref[...] = x_ref[...]
    for move in moves:
        move.wait()


def long_kernel(p_area, places, *refs):
    x_ref, columns_hbm, map_hbm, w_hbm, drive_hbm = refs[:5]
    w_ref, drive_ref, slots_ref, again_ref = refs[5:9]
    columns_ref, map_ref, wide_ref, sems, w_sems = refs[9:]
    p_dev = w_ref.shape[0]
    moves = [
        pltpu.make_async_copy(a, b, sems.at[n])
        for n, (a, b) in enumerate(
            ((columns_hbm, columns_ref), (map_hbm, map_ref), (drive_hbm, drive_ref))
        )
    ]
    for move in moves:
        move.start()
    w_moves = pieces(w_hbm, wide_ref, p_dev, w_sems)
    again_ref[...] = x_ref[...]
    for p, move in enumerate(w_moves):
        move.wait()
        for k in range(w_ref.shape[1]):
            w_ref[p, k] = wide_ref[p, k].T
    for move in moves:
        move.wait()
    area, local = lax.axis_index("area"), lax.axis_index("local")
    inside_bits = log2(p_area)
    columns = columns_ref[...]
    logical = columns >> inside_bits
    inside = columns & ((1 << inside_bits) - 1)
    target = jnp.zeros_like(columns)
    for a in range(map_ref.shape[0]):
        target = jnp.where(logical == a, map_ref[a], target)
    da = target ^ area
    dl = (inside >> log2(p_dev)) ^ local
    dc = da & (CORES - 1)
    away = (da >> log2(CORES)) * (p_area // p_dev) + dl
    place = jnp.zeros_like(columns)
    for core in range(CORES):
        held = ((target & (CORES - 1)) == core).astype(jnp.int32)
        for by, at in places[core].items():
            place = jnp.where((away == by) & (held == 1), at, place)
    place = dc * len(places[0]) + place
    slots_ref[...] = place * p_dev + (inside & (p_dev - 1))


def count_of(counts_ref, area):
    count = counts_ref[0]
    for a in range(1, counts_ref.shape[0]):
        count = jnp.where(area == a, counts_ref[a], count)
    return count


def round_kernel(p_dev, x_ref, counts_ref, out_ref, wide_ref, count_ref, sems):
    half = x_ref.shape[0] // 2
    parts = [pl.ds(n * half, half) for n in range(2)]
    moves = [
        pltpu.make_async_copy(x_ref.at[at], wide_ref.at[at], sems.at[n])
        for n, at in enumerate(parts)
    ]
    small = pltpu.make_async_copy(counts_ref, count_ref, sems.at[2])
    small.start()
    for move in moves:
        move.start()
    small.wait()
    count = count_of(count_ref, lax.axis_index("area"))
    first = lax.axis_index("local") * p_dev
    pop = x_ref.shape[1] // p_dev
    for move, at in zip(moves, parts):
        move.wait()
        for s in range(p_dev):
            here = slice(s * pop, (s + 1) * pop)
            x = wide_ref[at, here]
            out_ref[at, here] = jnp.where(
                first + s < count, x, jnp.zeros_like(x)
            ).astype(out_ref.dtype)


def column_kernel(*refs):
    out_ref = refs[-1]
    cond = refs[0].shape[0]
    for d, block in enumerate(refs[:-1]):
        out_ref[d * cond : (d + 1) * cond, :] = block[...]


def lay(arrays, table, start, cond):
    pop = table.shape[2]
    at = start
    for a in arrays:
        for d in range(a.shape[0] // cond):
            for s in range(a.shape[1] // pop):
                table[at] = a[d * cond : (d + 1) * cond, s * pop : (s + 1) * pop]
                at += 1


def add_inner(lists, cond, arrays, w_ref, start_ref, out_ref):
    here = lax.axis_index("local")
    width = out_ref.shape[1]

    def add(blocks):
        total = None if start_ref is None else start_ref[...]
        for n, d, far in blocks:
            at = pl.ds(pl.multiple_of((here ^ far) * width, width), width)
            part = lax.dot_general(
                arrays[n][d * cond : (d + 1) * cond, :],
                w_ref[:, at],
                DIMS,
                preferred_element_type=jnp.float32,
            )
            total = part if total is None else total + part
        out_ref[...] = total

    if lists[0] == lists[1]:
        add(lists[0])
        return
    odd = lax.axis_index("area") & 1
    for core in range(CORES):
        pl.when(odd == core)(functools.partial(add, lists[core]))


def inner_kernel(lists, cond, blocks_ref, w_ref, out_ref, again_ref):
    again_ref[...] = blocks_ref[...]
    add_inner(lists, cond, [blocks_ref], w_ref, None, out_ref)


def rest_kernel(lists, cond, w_ref, start_ref, *refs):
    arrays, out_ref, table = refs[:-2], refs[-2], refs[-1]
    lay(arrays, table, 0, cond)
    add_inner(lists, cond, arrays, w_ref, start_ref, out_ref)


def outer_kernel(start, *refs):
    counts_ref, slots_ref, w_ref, inner_ref, drive_ref = refs[:5]
    arrays, out_ref, table = refs[5:-3], refs[-2], refs[-1]
    p_dev, kblk, pop, _ = w_ref.shape
    lay(arrays, table, start, out_ref.shape[0])
    count = count_of(counts_ref, lax.axis_index("area"))
    first = lax.axis_index("local") * p_dev
    for p in range(p_dev):
        picked = jnp.concatenate([table[slots_ref[p, k]] for k in range(kblk)], axis=1)
        weights = w_ref[p].reshape(kblk * pop, pop)
        outer = jnp.dot(picked, weights, preferred_element_type=jnp.float32)
        here = slice(p * pop, (p + 1) * pop)
        rates = jnp.tanh(inner_ref[:, here] + outer + drive_ref[:, here])
        present = jnp.where(first + p < count, 1.0, 0.0)
        out_ref[:, here] = (rates * present).astype(out_ref.dtype)


def plan(nx, l1, l2):
    line = [(0, d * l2) for d in range(l1)]
    plane = [(dx, d2) for dx in range(nx) for d2 in range(l2)]
    if len(line) != len(plane):
        return [(a, a) for a in line], [(a, a) for a in plane]
    first = [(line[a], plane[b]) for a, b in FIRST]
    second = [(plane[a], line[b]) for a, b in SECOND]
    return first, second


def body(rates_init, drive, within_w, long_w, columns, area_map, counts):
    areas, locs = lax.axis_size("area"), lax.axis_size("local")
    nx, l1 = areas // CORES, 4
    l2 = locs // l1
    p_dev, kblk, pop, _ = long_w.shape
    cond, width = rates_init.shape
    devices = areas * locs
    first, second = plan(nx, l1, l2)
    places = [{}, {}]
    lists = [([], []), ([], [])]
    for core in range(CORES):
        for n, by_n in enumerate(second):
            for d, by_d in enumerate(first):
                dx = by_n[core][0] ^ by_d[core][0]
                dl = by_n[core][1] ^ by_d[core][1]
                places[core][dx * locs + dl] = n * len(first) + d
                if dx == 0:
                    lists[n > 0][core].append((n, d, dl))

    def swap(x, by):
        far = [dx * CORES * locs + dl for dx, dl in by]
        return lax.ppermute(
            x, AXES, [(i, i ^ far[(i // locs) % CORES]) for i in range(devices)]
        )

    def across(x):
        return lax.ppermute(x, AXES, [(i, i ^ locs) for i in range(devices)])

    shape = jax.ShapeDtypeStruct
    mine = call(
        functools.partial(round_kernel, p_dev),
        pltpu.VMEM(rates_init.shape, jnp.bfloat16),
        [in_hbm(rates_init), in_hbm(counts)],
        [HBM] * 2,
        0,
        scratch=[
            pltpu.VMEM(rates_init.shape, rates_init.dtype),
            pltpu.VMEM(counts.shape, counts.dtype),
            pltpu.SemaphoreType.DMA((3,)),
        ],
    )
    within_w, kept = call(
        within_kernel,
        [pltpu.VMEM(x.shape, x.dtype) for x in (within_w, mine)],
        [mine, in_hbm(within_w)],
        [VMEM, HBM],
        0,
        scratch=[pltpu.SemaphoreType.DMA((PIECES,))],
        out_specs=[VMEM] * 2,
    )
    for step in range(STEPS):
        column = call(
            column_kernel,
            shape((len(first) * cond, width), mine.dtype),
            [kept] + [swap(mine, by) for by in first[1:]],
            [VMEM] * len(first),
            0,
        )
        whole = column
        if step == 0:
            long_w, drive, slots, whole = call(
                functools.partial(long_kernel, locs * p_dev, places),
                [
                    pltpu.VMEM(x.shape, x.dtype)
                    for x in (long_w, drive, columns, column)
                ],
                [column] + [in_hbm(x) for x in (columns, area_map, long_w, drive)],
                [VMEM] + [HBM] * 4,
                0,
                scratch=[
                    pltpu.VMEM(columns.shape, columns.dtype),
                    pltpu.VMEM(area_map.shape, area_map.dtype),
                    pltpu.VMEM(long_w.shape, long_w.dtype),
                    pltpu.SemaphoreType.DMA((3,)),
                    pltpu.SemaphoreType.DMA((p_dev,)),
                ],
                out_specs=[VMEM] * 4,
            )
        partial = shape((cond, width), jnp.float32)
        flops = 2 * cond * width * width * l1
        inner, whole = call(
            functools.partial(inner_kernel, lists[0], cond),
            [partial, shape(column.shape, column.dtype)],
            (whole, within_w),
            [VMEM] * 2,
            flops,
            out_specs=[VMEM] * 2,
        )
        arrays = [whole] + [swap(column, by) for by in second[1:]]
        arrays += [across(x) for x in arrays]
        early = len(second) + 1
        per = len(first) * p_dev
        table = pltpu.VMEM((len(arrays) * per, cond, pop), mine.dtype)
        inner, picks = call(
            functools.partial(rest_kernel, lists[1], cond),
            [partial, table],
            [within_w, inner] + arrays[:early],
            [VMEM] * (2 + early),
            flops,
            out_specs=[VMEM] * 2,
        )
        operands = [counts, slots, long_w, inner, drive] + arrays[early:] + [picks]
        last = step == STEPS - 1
        mine, _ = call(
            functools.partial(outer_kernel, early * per),
            [shape((cond, width), jnp.float32 if last else jnp.bfloat16), table],
            operands,
            [VMEM] * len(operands),
            2 * cond * width * kblk * pop,
            out_specs=[VMEM] * 2,
            aliases={len(operands) - 1: 1},
        )
        kept = mine
    return mine


def solution(mesh):
    in_specs = (
        P(None, AXES),
        P(None, AXES),
        P(AXES, None),
        P(AXES, None, None, None),
        P(AXES, None),
        P(),
        P(),
    )
    return jax.shard_map(
        body, mesh=mesh, in_specs=in_specs, out_specs=P(None, AXES), check_vma=False
    )
```
